256 devices in a mesh: dp: 32 (over z, y_hi, core), tensor: 8 (over x, y_lo).
Axes of the slice: x: 4, y: 4 (y_hi: 2, y_lo: 2; y = y_hi * 2 + y_lo), z: 8, core: 2. Of those that a mesh axis runs over, the one named last changes fastest.
Arguments:
- layer_input: bfloat16 [512, 8192], P('dp', 'tensor'), may hold values from -6 to 6
- out_cotangent: bfloat16 [512, 8192], P('dp', 'tensor'), may hold values from -6 to 6
- old_gate: bfloat16 [8192, 16384], P('tensor', 'dp'), may hold values from -0.0625 to 0.0625
- old_up: bfloat16 [8192, 16384], P('tensor', 'dp'), may hold values from -0.0625 to 0.0625
- old_down: bfloat16 [8192, 16384], P('tensor', 'dp'), may hold values from -0.046875 to 0.046875
Outputs:
- layer_out: bfloat16 [512, 8192], P('dp', 'tensor')
- token_grad: bfloat16 [512, 8192], P('dp', 'tensor')
- gate_weight_grad: bfloat16 [4096, 32768], P('tensor', 'dp')
- up_weight_grad: bfloat16 [4096, 32768], P('tensor', 'dp')
- down_weight_grad: bfloat16 [4096, 32768], P('tensor', 'dp')
The draws below stay inside these ranges and needn't reach their ends.
All inputs are finite; a program needn't handle non-finite values.
Results may differ from the reference program's by a relative error of at most 0.02.
Values may be sent and summed in bfloat16 or wider, within the bound.
A program may use at most 64 MiB of HBM per device.

```python
import jax
import jax.numpy as jnp
from jax import lax

D = 8192
FF = 16384
TOKENS = 512
HALF_ROWS = 512
PAIR_COLS = 1024
N_DP = 32
N_TENSOR = 8


def levels(stream_key, shape, shards, least, high):
    level = 1.0
    for position, blocks in shards:
        heights = jax.random.uniform(jax.random.fold_in(jax.random.fold_in(stream_key, 6), position), (blocks,), jnp.float32, least / len(shards), high / len(shards))
        level = level * jnp.repeat(jnp.exp(heights), shape[position] // blocks).reshape((-1,) + (1,) * (len(shape) - 1 - position))
    return level


def noise(stream_key, dims, deviation, reach, cuts=(), held_as=jnp.bfloat16):
    entries = jax.random.normal(stream_key, dims, jnp.float32) * deviation
    if len(cuts) > 0:
        entries = levels(stream_key, dims, cuts, -0.22, 0.18) * entries
    return jnp.clip(entries, min=-reach, max=reach).astype(held_as)


def setup_inputs(seed: int = 0) -> dict:
    seeds = jax.random.split(jax.random.key(seed), 6)
    layer_input = noise(seeds[0], (TOKENS, D), 1.0, 6.0, ((0, 32), (1, 8)))
    out_cotangent = noise(seeds[1], (TOKENS, D), 1.0, 6.0, ((0, 32), (1, 8)))
    old_gate = noise(seeds[2], (D, FF), D ** -0.5, 0.0625, ((0, 8), (1, 32)))
    old_up = noise(seeds[3], (D, FF), D ** -0.5, 0.0625, ((0, 8), (1, 32)))
    old_down = noise(seeds[4], (D, FF), FF ** -0.5, 0.046875, ((0, 8), (1, 32)))
    return {"layer_input": layer_input, "out_cotangent": out_cotangent, "old_gate": old_gate, "old_up": old_up, "old_down": old_down}


def silu_parts(gate_value):
    sigma = jax.nn.sigmoid(gate_value)
    return gate_value * sigma, sigma * (1.0 + gate_value * (1.0 - sigma))


def new_storage(matrix):
    grid = matrix.reshape(N_TENSOR, 2, HALF_ROWS, N_DP // 2, PAIR_COLS)
    return grid.transpose(0, 2, 3, 1, 4).reshape(D // 2, 2 * FF)


def contract_rows(left, right):
    return lax.dot_general(left, right, (((0,), (0,)), ((), ())), preferred_element_type=jnp.float32)


def contract_cols(left, right):
    return lax.dot_general(left, right, (((1,), (1,)), ((), ())), preferred_element_type=jnp.float32)


def reference(layer_input, out_cotangent, old_gate, old_up, old_down):
    gate_value = jnp.dot(layer_input, old_gate, preferred_element_type=jnp.float32)
    up_value = jnp.dot(layer_input, old_up, preferred_element_type=jnp.float32)
    silu_value, silu_slope = silu_parts(gate_value)
    hidden = (silu_value * up_value).astype(jnp.bfloat16)
    layer_out = contract_cols(hidden, old_down).astype(jnp.bfloat16)
    hidden_grad = jnp.dot(out_cotangent, old_down, preferred_element_type=jnp.float32)
    gate_grad = (hidden_grad * up_value * silu_slope).astype(jnp.bfloat16)
    up_grad = (hidden_grad * silu_value).astype(jnp.bfloat16)
    down_weight_grad = new_storage(contract_rows(out_cotangent, hidden).astype(jnp.bfloat16))
    gate_weight_grad = new_storage(contract_rows(layer_input, gate_grad).astype(jnp.bfloat16))
    up_weight_grad = new_storage(contract_rows(layer_input, up_grad).astype(jnp.bfloat16))
    token_grad = (contract_cols(gate_grad, old_gate) + contract_cols(up_grad, old_up)).astype(jnp.bfloat16)
    return layer_out, token_grad, gate_weight_grad, up_weight_grad, down_weight_grad
```

```python
import functools
import itertools

import jax
import jax.numpy as jnp
from jax import lax
from jax.experimental import pallas as pl
from jax.experimental.pallas import tpu as pltpu
from jax.sharding import PartitionSpec as P

MESH = pl.DeviceIdType.MESH
F32 = jnp.float32
BF16 = jnp.bfloat16

ORDER = (0, 1, -1, 2, -2, 3, -3, 4)
CHUNKS = 4
COPIES = 288


def dot(a, b):
    return jnp.dot(a, b, preferred_element_type=F32)


def dot_cols(a, b):
    return lax.dot_general(a, b, (((1,), (1,)), ((), ())), preferred_element_type=F32)


def dot_rows(a, b):
    return lax.dot_general(a, b, (((0,), (0,)), ((), ())), preferred_element_type=F32)


def kernel(
    x_ref, c_ref, wg_any, wu_any, wd_any,
    lo_ref, tg_ref, gw_any, uw_any, dw_any,
    wg, wu, wd, xg, cg, part, got, hh, hs, mine, sib_out, sib_in, ring_out, ring_in, fin_out, fin, gw,
    wsem, osem, ssem, rsem,
):
    dp = lax.axis_index("dp")
    me = lax.axis_index("tensor")
    core, yh, z = dp % 2, (dp // 2) % 2, dp // 4
    x, yl = me // 2, me % 2
    tokens, width = x_ref.shape
    units = wg_any.shape[1]
    chunk = 8 * tokens

    def at(dz, flip_y=0, flip_core=0):
        return (((z + dz + 8) % 8) * 4 + ((yh + flip_y) % 2) * 2 + (core + flip_core) % 2, me)

    def tensor_index(j):
        jx = (x, x + 1 - 2 * (x % 2), (x + 2) % 4, 3 - x)[j // 2]
        return jx * 2 + (yl + j % 2) % 2

    sibling = at(0, 0, 1)
    loads = [
        pltpu.make_async_copy(src, dst, wsem.at[i])
        for i, (src, dst) in enumerate(((wg_any, wg), (wu_any, wu), (wd_any, wd)))
    ]
    for load in loads:
        load.start()

    barrier = pltpu.get_barrier_semaphore()
    peers = [at(1), at(-1), at(1, 1), at(-1, 1), at(0, 1), sibling]
    peers += [(dp, tensor_index(j)) for j in range(1, 8)]
    for peer in peers:
        pl.semaphore_signal(barrier, inc=1, device_id=peer, device_id_type=MESH)
    pl.semaphore_wait(barrier, len(peers))

    numbers = itertools.count()
    sent = []

    def send(src, dst, device):
        number = next(numbers)
        copy = pltpu.make_async_remote_copy(
            src_ref=src, dst_ref=dst, send_sem=ssem.at[number], recv_sem=rsem.at[number],
            device_id=device, device_id_type=MESH,
        )
        copy.start()
        sent.append(copy)
        return copy

    held = (xg, cg)
    own = (x_ref, c_ref)
    due = {}

    def block(a, d, s):
        return held[a].at[pl.ds((ORDER.index(d) * 4 + s) * tokens, tokens), :]

    def share(a, d, s):
        due[a, d, s + 1] = send(block(a, d, s), block(a, d, s + 1), sibling)

    for a in (0, 1):
        due[a, -1, 0] = send(own[a], block(a, -1, 0), at(1))
        due[a, 1, 0] = send(own[a], block(a, 1, 0), at(-1))
        due[a, -1, 2] = send(own[a], block(a, -1, 2), at(1, 1))
        due[a, 1, 2] = send(own[a], block(a, 1, 2), at(-1, 1))
        due[a, 0, 2] = send(own[a], block(a, 0, 2), at(0, 1))
        due[a, 0, 1] = send(own[a], block(a, 0, 1), sibling)
    for a in (0, 1):
        held[a][0:tokens, :] = own[a][...]

    def pass_on(a, d, s):
        if d == 4:
            due[a, 4, s].wait_recv()
            share(a, 4, s)
            return
        due[a, -d, s].wait_recv()
        if d < 3 or s == 0:
            far = -(d + 1) if d < 3 else 4
            due[a, far, s] = send(block(a, -d, s), block(a, far, s), at(1))
        share(a, -d, s)
        due[a, d, s].wait_recv()
        if d < 3 or s == 2:
            due[a, d + 1, s] = send(block(a, d, s), block(a, d + 1, s), at(-1))
        share(a, d, s)

    summed = {}

    def partial_sums(k):
        rows = pl.ds(k * chunk, chunk)
        for a in (0, 1):
            for d in ORDER[2 * k : 2 * k + 2]:
                for s in (1, 3):
                    due[a, d, s].wait_recv()
        for i, (values, weight) in enumerate(((xg, wg), (xg, wu), (cg, wd))):
            if k == 0:
                loads[i].wait()
            sums = dot(values[rows, :], weight[...]).astype(BF16)
            part[k, :, :, i * units : (i + 1) * units] = sums.reshape(8, tokens, units)
        for j in (4, 5, 2, 6, 3, 7, 1):
            summed[k, j] = send(part.at[k, tensor_index(j)], got.at[k, j], (dp, tensor_index(j)))

    for d in (1, 2, 3, 4):
        for s in (0, 2):
            for a in (0, 1):
                pass_on(a, d, s)
        if d == 1:
            for a in (0, 1):
                due[a, 0, 2].wait_recv()
                share(a, 0, 2)
        partial_sums(d - 1)

    spread = {}

    def finish_units(k):
        for j in range(1, 8):
            summed[k, j].wait_recv()
        total = part[k, me].astype(F32)
        for j in range(1, 8):
            total = total + got[k, j].astype(F32)
        gate, up, grad = (total[:, i * units : (i + 1) * units] for i in range(3))
        sigma = jax.nn.sigmoid(gate)
        silu = gate * sigma
        slope = sigma * (1.0 + gate * (1.0 - sigma))
        mine_now = hh.at[k, me // 2, me % 2]
        mine_now[:, 0:units] = (silu * up).astype(BF16)
        mine_now[:, units : 2 * units] = (grad * up * slope).astype(BF16)
        mine_now[:, 2 * units :] = (grad * silu).astype(BF16)
        for j in (4, 5, 2, 6, 3, 7, 1):
            spread[k, j] = send(mine_now, mine_now, (dp, tensor_index(j)))

    handed, lent = {}, []

    def output_terms(k):
        for j in range(1, 8):
            spread[k, j].wait_recv()
        lent.append(send(hh.at[k, :, 0], hs.at[k, :, 1], sibling))
        lent.append(send(hh.at[k, :, 1], hs.at[k, :, 0], sibling))
        values = hh[k].reshape(chunk, 3 * units)
        out = dot_cols(values[:, 0:units], wd[...])
        grad = dot_cols(values[:, units : 2 * units], wg[...]) + dot_cols(values[:, 2 * units :], wu[...])
        for i, term in enumerate((out, grad)):
            term = term.reshape(2, 2, 2, tokens, width)
            mine[k, :, :, :, i * width : (i + 1) * width] = term[:, :, 0]
            sib_out[k, :, :, :, i * width : (i + 1) * width] = term[:, :, 1].astype(BF16)
        handed[k] = send(sib_out.at[k], sib_in.at[k], sibling)

    def reduced(d):
        slot = ORDER.index(d)
        return mine[slot // 2, slot % 2] + sib_in[slot // 2, slot % 2].astype(F32)

    rung = {}

    def step(d, way):
        slot = ORDER.index(d)
        value = reduced(d)
        if d == 4:
            half = 0 if way > 0 else 1
            ring_out[slot, half] = value[half].astype(BF16)
            to = ORDER.index(3 * way)
            rung[3 * way] = send(ring_out.at[slot, half], ring_in.at[to, half], at(way))
            return
        rung[d].wait_recv()
        if abs(d) == 3:
            half = 0 if way > 0 else 1
            first = value[0] + ring_in[slot, 0].astype(F32) if half == 0 else value[0]
            second = value[1] + ring_in[slot, 1].astype(F32) if half == 1 else value[1]
        else:
            first = value[0] + ring_in[slot, 0].astype(F32)
            second = value[1] + ring_in[slot, 1].astype(F32)
        ring_out[slot, 0] = first.astype(BF16)
        ring_out[slot, 1] = second.astype(BF16)
        if abs(d) == 1:
            place = 0 if way > 0 else 2
            rung["end", place] = send(ring_out.at[slot, 0], fin.at[place], at(way))
            rung["end", place + 1] = send(ring_out.at[slot, 1], fin.at[place + 1], at(way, 1))
        else:
            to = ORDER.index(d - way)
            rung[d - way] = send(ring_out.at[slot], ring_in.at[to], at(way))

    finish_units(2)
    finish_units(3)
    finish_units(1)
    finish_units(0)
    output_terms(2)
    output_terms(3)
    handed[3].wait_recv()
    step(4, 1)
    step(4, -1)
    output_terms(1)
    handed[2].wait_recv()
    step(-3, -1)
    step(3, 1)
    output_terms(0)
    handed[1].wait_recv()
    step(-2, -1)
    step(2, 1)
    handed[0].wait_recv()
    last = reduced(0)
    fin_out[...] = last[1].astype(BF16)
    rung["end", 4] = send(fin_out, fin.at[4], at(0, 1))
    step(-1, -1)
    step(1, 1)

    for copy in lent:
        copy.wait_recv()
    rows_all = CHUNKS * chunk
    half_width = width // 2
    tile = 128
    here = pl.multiple_of(core * units, units)
    there = pl.multiple_of((1 - core) * units, units)

    def weight_tile(i, carry):
        at_col = pl.multiple_of(core * half_width + i * tile, tile)
        at_row = pl.multiple_of(i * tile, tile)
        for m, values in enumerate((cg, xg, xg)):
            left = values[:, pl.ds(at_col, tile)]
            for source, place in ((hh, here), (hs, there)):
                right = source[:, :, :, :, m * units : (m + 1) * units].reshape(rows_all, units)
                gw[m, pl.ds(at_row, tile), pl.ds(place, units)] = dot_rows(left, right).astype(BF16)
        return carry

    lax.fori_loop(0, half_width // tile, weight_tile, 0)
    stores = [
        pltpu.make_async_copy(gw.at[m], dst, osem.at[m]) for m, dst in enumerate((dw_any, gw_any, uw_any))
    ]
    for store in stores:
        store.start()

    total = last[0]
    for place in range(5):
        rung["end", place].wait_recv()
        total = total + fin[place].astype(F32)
    lo_ref[...] = total[:, 0:width].astype(BF16)
    tg_ref[...] = total[:, width:].astype(BF16)
    for copy in sent:
        copy.wait_send()
    for store in stores:
        store.wait()


def shards(layer_input, out_cotangent, old_gate, old_up, old_down):
    tokens, width = layer_input.shape
    units = old_gate.shape[1]
    all_tokens = 32 * tokens
    vmem = pl.BlockSpec(memory_space=pltpu.VMEM)
    any_space = pl.BlockSpec(memory_space=pl.ANY)
    grad_shape = jax.ShapeDtypeStruct((width // 2, 2 * units), BF16)
    out_shape = jax.ShapeDtypeStruct((tokens, width), BF16)
    lo, tg, gw, uw, dw = pl.pallas_call(
        kernel,
        out_shape=(out_shape, out_shape, grad_shape, grad_shape, grad_shape),
        in_specs=[vmem, vmem, any_space, any_space, any_space],
        out_specs=[vmem, vmem, any_space, any_space, any_space],
        scratch_shapes=[
            pltpu.VMEM((width, units), BF16),
            pltpu.VMEM((width, units), BF16),
            pltpu.VMEM((width, units), BF16),
            pltpu.VMEM((all_tokens, width), BF16),
            pltpu.VMEM((all_tokens, width), BF16),
            pltpu.VMEM((CHUNKS, 8, tokens, 3 * units), BF16),
            pltpu.VMEM((CHUNKS, 8, tokens, 3 * units), BF16),
            pltpu.VMEM((CHUNKS, 4, 2, tokens, 3 * units), BF16),
            pltpu.VMEM((CHUNKS, 4, 2, tokens, 3 * units), BF16),
            pltpu.VMEM((CHUNKS, 2, 2, tokens, 2 * width), F32),
            pltpu.VMEM((CHUNKS, 2, 2, tokens, 2 * width), BF16),
            pltpu.VMEM((CHUNKS, 2, 2, tokens, 2 * width), BF16),
            pltpu.VMEM((8, 2, tokens, 2 * width), BF16),
            pltpu.VMEM((8, 2, tokens, 2 * width), BF16),
            pltpu.VMEM((tokens, 2 * width), BF16),
            pltpu.VMEM((5, tokens, 2 * width), BF16),
            pltpu.VMEM((3, width // 2, 2 * units), BF16),
            pltpu.SemaphoreType.DMA((3,)),
            pltpu.SemaphoreType.DMA((3,)),
            pltpu.SemaphoreType.DMA((COPIES,)),
            pltpu.SemaphoreType.DMA((COPIES,)),
        ],
        compiler_params=pltpu.CompilerParams(
            collective_id=0, has_side_effects=True, vmem_limit_bytes=48 * 1024 * 1024
        ),
        cost_estimate=pl.CostEstimate(
            flops=18 * all_tokens * width * units, bytes_accessed=12 * width * units, transcendentals=0
        ),
    )(layer_input, out_cotangent, old_gate, old_up, old_down)
    return lo, tg, gw, uw, dw


def solution(mesh):
    wide = P("dp", "tensor")
    stored = P("tensor", "dp")
    return jax.shard_map(
        shards,
        mesh=mesh,
        in_specs=(wide, wide, stored, stored, stored),
        out_specs=(wide, wide, stored, stored, stored),
        check_vma=False,
    )
```

```python
import jax
import jax.numpy as jnp
from jax import lax
from jax.experimental import pallas as pl
from jax.experimental.pallas import tpu as pltpu
from jax.sharding import PartitionSpec as P

MESH = pl.DeviceIdType.MESH
F32 = jnp.float32
BF16 = jnp.bfloat16

ORDER = (0, 1, -1, 2, -2, 3, -3, 4)
CHUNKS = 4
SENDS, RECEIVES = 7, 57
ENDS = ((2, 0), (2, 1), (-2, 0), (-2, 1), (1, 0), (1, 1), (-1, 0), (-1, 1), (0, 1))


def dot(a, b):
    return jnp.dot(a, b, preferred_element_type=F32)


def dot_cols(a, b):
    return lax.dot_general(a, b, (((1,), (1,)), ((), ())), preferred_element_type=F32)


def dot_rows(a, b):
    return lax.dot_general(a, b, (((0,), (0,)), ((), ())), preferred_element_type=F32)


def kernel(
    x_ref, c_ref, wg_any, wu_any, wd_any,
    lo_ref, tg_ref, gw_out,
    wg, wu, wd, xg, cg, part, got, hh, hs, mine, sib_out, sib_in, sums_out, met_in, fin, gw,
    wsem, osem, ssem, rsem,
):
    dp = lax.axis_index("dp")
    me = lax.axis_index("tensor")
    core, yh, z = dp % 2, (dp // 2) % 2, dp // 4
    x, yl = me // 2, me % 2
    tokens, width = x_ref.shape
    units = wg_any.shape[1]
    chunk = 8 * tokens

    def at(dz, flip_y=0, flip_core=0):
        return (((z + dz + 8) % 8) * 4 + ((yh + flip_y) % 2) * 2 + (core + flip_core) % 2, me)

    def tensor_index(j):
        jx = (x, x + 1 - 2 * (x % 2), (x + 2) % 4, 3 - x)[j // 2]
        return jx * 2 + (yl + j % 2) % 2

    sibling = at(0, 0, 1)
    loads = [
        pltpu.make_async_copy(src, dst, wsem.at[i])
        for i, (src, dst) in enumerate(((wg_any, wg), (wu_any, wu), (wd_any, wd)))
    ]
    mine_in = [
        pltpu.make_async_copy(src, dst.at[pl.ds(0, tokens), :], wsem.at[3 + i])
        for i, (src, dst) in enumerate(((x_ref, xg), (c_ref, cg)))
    ]
    for load in mine_in + loads:
        load.start()

    barrier = pltpu.get_barrier_semaphore()
    peers = [at(1), at(-1), at(1, 1), at(-1, 1), at(0, 1), sibling]
    peers += [at(2), at(-2), at(2, 1), at(-2, 1)]
    peers += [(dp, tensor_index(j)) for j in range(1, 8)]
    for peer in peers:
        pl.semaphore_signal(barrier, inc=1, device_id=peer, device_id_type=MESH)
    pl.semaphore_wait(barrier, len(peers))

    places = {}

    def place_of(kind, key):
        return places.setdefault((kind, key), sum(1 for k, _ in places if k == kind))

    def send(src, dst, device, key, group):
        copy = pltpu.make_async_remote_copy(
            src_ref=src, dst_ref=dst, send_sem=ssem.at[place_of("send", group)], recv_sem=rsem.at[place_of("recv", key)],
            device_id=device, device_id_type=MESH,
        )
        copy.start()

    def of_size(ref, key, group):
        return pltpu.make_async_remote_copy(
            src_ref=ref, dst_ref=ref, send_sem=ssem.at[place_of("send", group)], recv_sem=rsem.at[place_of("recv", key)],
            device_id=sibling, device_id_type=MESH,
        )

    def arrived(ref, *key):
        of_size(ref, key, "gather0").wait_recv()

    def left(ref, group):
        of_size(ref, ("gather", 0, 1, 0), group).wait_send()

    held = (xg, cg)
    own = (x_ref, c_ref)

    def block(a, d, s):
        return held[a].at[pl.ds((ORDER.index(d) * 4 + s) * tokens, tokens), :]

    def pass_to(a, src, d, s, device):
        send(src, block(a, d, s), device, ("gather", a, d, s), f"gather{a}")

    def share(a, src, d, s):
        send(src, block(a, d, s + 1), sibling, ("share", ORDER.index(d) // 2), f"gather{a}")

    def here_now(a, d, s):
        arrived(block(a, d, s), "gather", a, d, s)

    for a in (0, 1):
        pass_to(a, own[a], -1, 0, at(1))
        pass_to(a, own[a], 1, 0, at(-1))
        pass_to(a, own[a], -1, 2, at(1, 1))
        pass_to(a, own[a], 1, 2, at(-1, 1))
        pass_to(a, own[a], 0, 2, at(0, 1))
        share(a, own[a], 0, 0)

    def pass_on(a, d, s):
        for way in (1, -1):
            to = -way * d if d < 4 else 4
            if d == 4 and (way > 0) != (s == 0):
                continue
            here_now(a, to, s)
            if d < 3:
                pass_to(a, block(a, to, s), to - way, s, at(way))
            elif d == 3 and (way > 0) == (s == 0):
                pass_to(a, block(a, to, s), 4, s, at(way))
            share(a, block(a, to, s), to, s)

    def partial_sums(k):
        rows = pl.ds(k * chunk, chunk)
        arrived(xg.at[rows, :], "share", k)
        if k == 0:
            for load in mine_in + loads:
                load.wait()
        for i, (values, weight) in enumerate(((xg, wg), (xg, wu), (cg, wd))):
            sums = dot(values[rows, :], weight[...]).astype(BF16)
            part[k, :, :, i * units : (i + 1) * units] = sums.reshape(8, tokens, units)
        for j in (4, 5, 2, 6, 3, 7, 1):
            send(part.at[k, tensor_index(j)], got.at[k, j], (dp, tensor_index(j)), ("sums", k), "sums")

    for d in (1, 2, 3, 4):
        for s in (0, 2):
            for a in (0, 1):
                pass_on(a, d, s)
        if d == 1:
            for a in (0, 1):
                here_now(a, 0, 2)
                share(a, block(a, 0, 2), 0, 2)
        partial_sums(d - 1)

    def finish_units(k):
        arrived(got.at[k, pl.ds(1, 7)], "sums", k)
        total = part[k, me].astype(F32)
        for j in range(1, 8):
            total = total + got[k, j].astype(F32)
        gate, up, grad = (total[:, i * units : (i + 1) * units] for i in range(3))
        sigma = jax.nn.sigmoid(gate)
        silu = gate * sigma
        slope = sigma * (1.0 + gate * (1.0 - sigma))
        mine_now = hh.at[k, me // 2, me % 2]
        mine_now[:, 0:units] = (silu * up).astype(BF16)
        mine_now[:, units : 2 * units] = (grad * up * slope).astype(BF16)
        mine_now[:, 2 * units :] = (grad * silu).astype(BF16)
        for j in (4, 5, 2, 6, 3, 7, 1):
            send(mine_now, mine_now, (dp, tensor_index(j)), ("spread", k), "spread")

    def output_terms(k):
        arrived(got.at[k, pl.ds(1, 7)], "spread", k)
        send(hh.at[k, :, 0], hs.at[k, :, 1], sibling, ("lent",), "lent")
        send(hh.at[k, :, 1], hs.at[k, :, 0], sibling, ("lent",), "lent")
        values = hh[k].reshape(chunk, 3 * units)
        for half in (0, 1):
            if half == 0:
                term = dot_cols(values[:, 0:units], wd[...])
            else:
                term = dot_cols(values[:, units : 2 * units], wg[...])
                term = term + dot_cols(values[:, 2 * units :], wu[...])
            term = term.reshape(2, 2, 2, tokens, width)
            mine[k, half] = term[:, :, 0]
            sib_out[k, half] = term[:, :, 1].astype(BF16)
            send(sib_out.at[k, half], sib_in.at[k, half], sibling, ("handed", k, half), "handed")

    def reduced(d, half):
        k, i = ORDER.index(d) // 2, ORDER.index(d) % 2
        return mine[k, half, i] + sib_in[k, half, i].astype(F32)

    def step(d, half):
        value = reduced(d, half)
        way = 1 if d > 0 else -1
        out = sums_out.at[half, ORDER.index(d)]
        if abs(d) == 2:
            side = 0 if way > 0 else 1
            arrived(met_in.at[half, side], "met", half, side)
            value = value + met_in[half, side, 0:2].astype(F32)
            far = met_in[half, side, 2].astype(F32)
            out[side] = (value[side] + far).astype(BF16)
            out[1 - side] = value[1 - side].astype(BF16)
        else:
            out[...] = value.astype(BF16)
        if d == 4:
            send(out.at[0], met_in.at[half, 0, 2], at(2), ("met", half, 0), "output")
            send(out.at[1], met_in.at[half, 1, 2], at(-2), ("met", half, 1), "output")
        elif abs(d) == 3:
            side = 0 if way > 0 else 1
            send(out, met_in.at[half, side, pl.ds(0, 2)], at(way), ("met", half, side), "output")
        else:
            for s in (0, 1):
                place = ENDS.index((d, s)) if d or s else None
                if place is not None:
                    send(out.at[s], fin.at[half, place], at(d, s), ("ended", half), "output")

    finish_units(2)
    finish_units(3)
    finish_units(1)
    finish_units(0)

    def ready(k, half, steps):
        arrived(sib_in.at[k, half], "handed", k, half)
        for d in steps:
            step(d, half)

    output_terms(2)
    output_terms(3)
    for half in (0, 1):
        ready(2, half, (3,))
    for half in (0, 1):
        ready(3, half, (4, -3))
    output_terms(1)
    for half in (0, 1):
        step(-2, half)
        ready(1, half, (-1, 2))
    output_terms(0)
    for half in (0, 1):
        ready(0, half, (1, 0))

    arrived(hs, "lent")
    rows_all = CHUNKS * chunk
    half_width = width // 2
    tile = 128
    here = pl.multiple_of(core * units, units)
    there = pl.multiple_of((1 - core) * units, units)
    stores = []
    for m, values in enumerate((cg, xg, xg)):

        def weight_tile(i, carry):
            at_col = pl.multiple_of(core * half_width + i * tile, tile)
            at_row = pl.multiple_of(i * tile, tile)
            left = values[:, pl.ds(at_col, tile)]
            for source, place in ((hh, here), (hs, there)):
                right = source[:, :, :, :, m * units : (m + 1) * units].reshape(rows_all, units)
                gw[m, pl.ds(at_row, tile), pl.ds(place, units)] = dot_rows(left, right).astype(BF16)
            return carry

        lax.fori_loop(0, half_width // tile, weight_tile, 0)
        stores.append(pltpu.make_async_copy(gw.at[m], gw_out.at[m], osem.at[m]))
        stores[m].start()

    for half, out_ref in enumerate((lo_ref, tg_ref)):
        arrived(fin.at[half], "ended", half)
        total = mine[0, half, 0, 0] + sib_in[0, half, 0, 0].astype(F32)
        for place in range(len(ENDS)):
            total = total + fin[half, place].astype(F32)
        out_ref[...] = total.astype(BF16)
    for a in (0, 1):
        left(xg.at[pl.ds(0, 31 * tokens), :], f"gather{a}")
    left(got.at[:, pl.ds(1, 7)], "sums")
    left(got.at[:, pl.ds(1, 7)], "spread")
    left(hs, "lent")
    left(sib_in, "handed")
    left(xg.at[pl.ds(0, 30 * tokens), :], "output")
    for store in stores:
        store.wait()


def store_results(lo, tg, gw, lo_out, tg_out, gate_out, up_out, down_out, stage, in_sem, out_sem):
    rows = gw.shape[1] // 2
    loads, copies = [], []
    for m, out in enumerate((down_out, gate_out, up_out)):
        for i in range(2):
            part = pl.ds(i * rows, rows)
            n = 2 * m + i
            loads.append(pltpu.make_async_copy(gw.at[m, part], stage.at[m, part], in_sem.at[n]))
            copies.append(pltpu.make_async_copy(stage.at[m, part], out.at[part], out_sem.at[n]))
    ends = [
        pltpu.make_async_copy(src, dst, out_sem.at[6 + i])
        for i, (src, dst) in enumerate(((lo, lo_out), (tg, tg_out)))
    ]
    for copy in loads + ends:
        copy.start()
    for load, copy in zip(loads, copies):
        load.wait()
        copy.start()
    for copy in copies + ends:
        copy.wait()


def shards(layer_input, out_cotangent, old_gate, old_up, old_down):
    tokens, width = layer_input.shape
    units = old_gate.shape[1]
    all_tokens = 32 * tokens
    vmem = pl.BlockSpec(memory_space=pltpu.VMEM)
    hbm = pl.BlockSpec(memory_space=pltpu.HBM)
    grad_shape = jax.ShapeDtypeStruct((width // 2, 2 * units), BF16)
    out_shape = jax.ShapeDtypeStruct((tokens, width), BF16)
    results = pl.pallas_call(
        kernel,
        out_shape=(out_shape, out_shape, jax.ShapeDtypeStruct((3,) + grad_shape.shape, BF16)),
        in_specs=[hbm] * 5,
        out_specs=[vmem, vmem, hbm],
        scratch_shapes=[
            pltpu.VMEM((width, units), BF16),
            pltpu.VMEM((width, units), BF16),
            pltpu.VMEM((width, units), BF16),
            pltpu.VMEM((all_tokens, width), BF16),
            pltpu.VMEM((all_tokens, width), BF16),
            pltpu.VMEM((CHUNKS, 8, tokens, 3 * units), BF16),
            pltpu.VMEM((CHUNKS, 8, tokens, 3 * units), BF16),
            pltpu.VMEM((CHUNKS, 4, 2, tokens, 3 * units), BF16),
            pltpu.VMEM((CHUNKS, 4, 2, tokens, 3 * units), BF16),
            pltpu.VMEM((CHUNKS, 2, 2, 2, tokens, width), F32),
            pltpu.VMEM((CHUNKS, 2, 2, 2, tokens, width), BF16),
            pltpu.VMEM((CHUNKS, 2, 2, 2, tokens, width), BF16),
            pltpu.VMEM((2, 8, 2, tokens, width), BF16),
            pltpu.VMEM((2, 2, 3, tokens, width), BF16),
            pltpu.VMEM((2, len(ENDS), tokens, width), BF16),
            pltpu.VMEM((3, width // 2, 2 * units), BF16),
            pltpu.SemaphoreType.DMA((5,)),
            pltpu.SemaphoreType.DMA((3,)),
            pltpu.SemaphoreType.DMA((SENDS,)),
            pltpu.SemaphoreType.DMA((RECEIVES,)),
        ],
        compiler_params=pltpu.CompilerParams(
            collective_id=0, has_side_effects=True, vmem_limit_bytes=63 * 1024 * 1024
        ),
        cost_estimate=pl.CostEstimate(
            flops=18 * all_tokens * width * units, bytes_accessed=12 * width * units, transcendentals=0
        ),
    )(layer_input, out_cotangent, old_gate, old_up, old_down)
    return pl.pallas_call(
        store_results,
        out_shape=(out_shape, out_shape, grad_shape, grad_shape, grad_shape),
        in_specs=[vmem, vmem, hbm],
        out_specs=[hbm] * 5,
        scratch_shapes=[
            pltpu.VMEM((3,) + grad_shape.shape, BF16),
            pltpu.SemaphoreType.DMA((6,)),
            pltpu.SemaphoreType.DMA((8,)),
        ],
        compiler_params=pltpu.CompilerParams(vmem_limit_bytes=63 * 1024 * 1024),
    )(*results)


def solution(mesh):
    wide = P("dp", "tensor")
    stored = P("tensor", "dp")
    return jax.shard_map(
        shards,
        mesh=mesh,
        in_specs=(wide, wide, stored, stored, stored),
        out_specs=(wide, wide, stored, stored, stored),
        check_vma=False,
    )
```

```python
import jax
import jax.numpy as jnp
from jax import lax
from jax.experimental import pallas as pl
from jax.experimental.pallas import tpu as pltpu
from jax.sharding import PartitionSpec as P

MESH = pl.DeviceIdType.MESH
F32 = jnp.float32
BF16 = jnp.bfloat16

ENTRIES = (
    (0, 0), (0, 1), (1, 0), (-1, 0),
    (1, 1), (-1, 1), (2, 0), (-2, 0),
    (2, 1), (-2, 1), (3, 1), (-3, 0),
    (3, 0), (-3, 1), (4, 0), (4, 1),
)
CHUNKS = 4
DIRECT = (1, 2, 3)
SENDS, RECEIVES = 12, 30 + 8 + 4 * (CHUNKS - len(DIRECT)) + len(DIRECT) + 23
CUT = 640
FIRST, SECOND = pl.ds(0, CUT), pl.ds(CUT, 1536 - CUT)
ENDS = ((2, 0), (-2, 1), (1, 0), (1, 1), (-1, 0), (-1, 1), (0, 1))


def dot(a, b):
    return jnp.dot(a, b, preferred_element_type=F32)


def dot_cols(a, b):
    return lax.dot_general(a, b, (((1,), (1,)), ((), ())), preferred_element_type=F32)


def dot_rows(a, b):
    return lax.dot_general(a, b, (((0,), (0,)), ((), ())), preferred_element_type=F32)


def kernel(
    x_ref, c_ref, wg_any, wu_any, wd_any,
    lo_ref, tg_ref, gw_out,
    wg, wu, wd, xg, cg, part, in_x, in_y, out_x, out_y, end_x, end_y, kept, got, hh, hs, mine, sib_out, sib_in, sums_out, met_in, fin, gw,
    wsem, osem, ssem, rsem,
):
    dp = lax.axis_index("dp")
    me = lax.axis_index("tensor")
    core, yh, z = dp % 2, (dp // 2) % 2, dp // 4
    x, yl = me // 2, me % 2
    tokens, width = x_ref.shape
    units = wg_any.shape[1]
    chunk = 8 * tokens

    def at(dz, flip_y=0, flip_core=0):
        return (((z + dz + 8) % 8) * 4 + ((yh + flip_y) % 2) * 2 + (core + flip_core) % 2, me)

    def x_of(j):
        return (x, x + 1 - 2 * (x % 2), (x + 2) % 4, 3 - x)[j]

    def peer_of(j):
        return (dp, x_of(j // 2) * 2 + (yl + j % 2) % 2)

    def x_peer(j):
        return peer_of(2 * j)

    y_peer = peer_of(1)
    sibling = at(0, 0, 1)
    loads = [
        pltpu.make_async_copy(src, dst, wsem.at[i])
        for i, (src, dst) in enumerate(((wg_any, wg), (wu_any, wu), (wd_any, wd)))
    ]
    mine_in = [
        pltpu.make_async_copy(src, dst.at[pl.ds(0, tokens), :], wsem.at[3 + i])
        for i, (src, dst) in enumerate(((x_ref, xg), (c_ref, cg)))
    ]
    for load in mine_in + loads:
        load.start()

    barrier = pltpu.get_barrier_semaphore()
    peers = [at(1), at(-1), at(1, 1), at(-1, 1), at(0, 1), sibling]
    peers += [at(2), at(-2), at(2, 1), at(-2, 1)]
    peers += [peer_of(j) for j in range(1, 8)]
    for peer in peers:
        pl.semaphore_signal(barrier, inc=1, device_id=peer, device_id_type=MESH)
    pl.semaphore_wait(barrier, len(peers))

    places = {}

    def place_of(kind, key):
        return places.setdefault((kind, key), sum(1 for k, _ in places if k == kind))

    def send(src, dst, device, key, group):
        copy = pltpu.make_async_remote_copy(
            src_ref=src, dst_ref=dst, send_sem=ssem.at[place_of("send", group)], recv_sem=rsem.at[place_of("recv", key)],
            device_id=device, device_id_type=MESH,
        )
        copy.start()

    def of_size(ref, key, group):
        return pltpu.make_async_remote_copy(
            src_ref=ref, dst_ref=ref, send_sem=ssem.at[place_of("send", group)], recv_sem=rsem.at[place_of("recv", key)],
            device_id=sibling, device_id_type=MESH,
        )

    def arrived(ref, *key):
        of_size(ref, key, "gather0").wait_recv()

    def left(ref, group):
        of_size(ref, ("gather", 0, 1, 0), group).wait_send()

    held = (xg, cg)
    own = (x_ref, c_ref)

    def block(a, d, s):
        return held[a].at[pl.ds((ENTRIES.index((d, s // 2)) * 2 + s % 2) * tokens, tokens), :]

    def pass_to(a, src, d, s, device):
        send(src, block(a, d, s), device, ("gather", a, d, s), f"gather{a}")

    def share(a, src, d, s):
        send(src, block(a, d, s + 1), sibling, ("share", ENTRIES.index((d, s // 2)) // 4), f"gather{a}")

    def here_now(a, d, s):
        arrived(block(a, d, s), "gather", a, d, s)

    for a in (0, 1):
        pass_to(a, own[a], -1, 0, at(1))
        pass_to(a, own[a], 1, 0, at(-1))
        pass_to(a, own[a], -1, 2, at(1, 1))
        pass_to(a, own[a], 1, 2, at(-1, 1))
        pass_to(a, own[a], 0, 2, at(0, 1))
        share(a, own[a], 0, 0)

    def pass_on(a, d, s):
        for way in (1, -1):
            to = -way * d if d < 4 else 4
            if d == 4 and (way > 0) != (s == 0):
                continue
            here_now(a, to, s)
            if d < 3:
                pass_to(a, block(a, to, s), to - way, s, at(way))
            elif d == 3 and (way > 0) == (s == 0):
                pass_to(a, block(a, to, s), 4, s, at(way))
            share(a, block(a, to, s), to, s)

    def own_pair(a):
        here_now(a, 0, 2)
        share(a, block(a, 0, 2), 0, 2)

    def partial_sums(k):
        rows = pl.ds(k * chunk, chunk)
        arrived(xg.at[rows, :], "share", k)
        if k == 0:
            for load in mine_in + loads:
                load.wait()
        for i, (values, weight) in enumerate(((xg, wg), (xg, wu), (cg, wd))):
            sums = dot(values[rows, :], weight[...]).astype(BF16)
            part[k, :, :, :, i * units : (i + 1) * units] = sums.reshape(4, 2, tokens, units)
        if k in DIRECT:
            for j in (4, 5, 2, 6, 3, 7, 1):
                src = part.at[k, x_of(j // 2), (yl + j % 2) % 2]
                send(src, got.at[DIRECT.index(k), j - 1], peer_of(j), ("sums", k), "sums")
            return
        send(part.at[k, :, 1 - yl, :, SECOND], in_y.at[k], y_peer, ("sums y", k), "sums y")
        for j in (2, 1, 3):
            send(part.at[k, x_of(j), :, :, FIRST], in_x.at[k, j - 1], x_peer(j), ("sums x", k), "sums x")

    def mix_sums(k):
        arrived(in_y.at[k], "sums y", k)
        both = part[k, :, yl, :, SECOND].astype(F32) + in_y[k].astype(F32)
        out_y[k] = both.astype(BF16)
        for j in (2, 1, 3):
            send(out_y.at[k, x_of(j)], end_x.at[k, j - 1], x_peer(j), ("mixed x", k), "mixed x")
        arrived(in_x.at[k], "sums x", k)
        theirs, ours = part[k, x, 1 - yl, :, FIRST].astype(F32), part[k, x, yl, :, FIRST].astype(F32)
        for j in range(3):
            theirs = theirs + in_x[k, j, 1 - yl].astype(F32)
            ours = ours + in_x[k, j, yl].astype(F32)
        out_x[k] = theirs.astype(BF16)
        kept[k] = ours
        send(out_x.at[k], end_y.at[k], y_peer, ("mixed y", k), "mixed y")

    def finish_units(k):
        if k in DIRECT:
            mail = got.at[DIRECT.index(k)]
            arrived(mail, "sums", k)
            total = part[k, x, yl].astype(F32)
            for j in range(7):
                total = total + mail[j].astype(F32)
        else:
            arrived(end_x.at[k], "mixed x", k)
            arrived(end_y.at[k], "mixed y", k)
            first = kept[k] + end_y[k].astype(F32)
            second = out_y[k, x].astype(F32)
            for j in range(3):
                second = second + end_x[k, j].astype(F32)
            total = jnp.concatenate([first, second], axis=1)
        gate, up, grad = (total[:, i * units : (i + 1) * units] for i in range(3))
        sigma = jax.nn.sigmoid(gate)
        silu = gate * sigma
        slope = sigma * (1.0 + gate * (1.0 - sigma))
        mine_now = hh.at[k, x, yl]
        mine_now[:, 0:units] = (silu * up).astype(BF16)
        mine_now[:, units : 2 * units] = (grad * up * slope).astype(BF16)
        mine_now[:, 2 * units :] = (grad * silu).astype(BF16)
        for j in (4, 5, 2, 6, 3, 7, 1):
            send(mine_now, mine_now, peer_of(j), ("spread", k), "spread last" if j == 1 else "spread")

    def output_terms(k):
        arrived(got.at[0], "spread", k)
        send(hh.at[k, :, 0], hs.at[k, :, 1], sibling, ("lent",), "lent")
        send(hh.at[k, :, 1], hs.at[k, :, 0], sibling, ("lent",), "lent")
        values = hh[k].reshape(chunk, 3 * units)
        for half in (0, 1):
            if half == 0:
                term = dot_cols(values[:, 0:units], wd[...])
            else:
                term = dot_cols(values[:, units : 2 * units], wg[...])
                term = term + dot_cols(values[:, 2 * units :], wu[...])
            term = term.reshape(4, 2, tokens, width)
            mine[k, half] = term[:, 0]
            sib_out[k, half] = term[:, 1].astype(BF16)
            send(sib_out.at[k, half], sib_in.at[k, half], sibling, ("handed", k, half), "handed")

    def step(d, h, half):
        entry = ENTRIES.index((d, h))
        value = mine[entry // 4, half, entry % 4] + sib_in[entry // 4, half, entry % 4].astype(F32)
        side = 0 if d > 0 else 1
        out = sums_out.at[half, entry]
        if abs(d) == 2 and h == side:
            arrived(met_in.at[half, side, pl.ds(0, 2)], "met", half, side, h)
            value = value + met_in[half, side, 0].astype(F32) + met_in[half, side, 1].astype(F32)
        elif abs(d) == 2:
            arrived(met_in.at[half, side, 2], "met", half, side, h)
            value = value + met_in[half, side, 2].astype(F32)
        elif abs(d) == 1 and h != side:
            arrived(met_in.at[half, side, 3], "near", half, side)
            value = value + met_in[half, side, 3].astype(F32)
        out[...] = value.astype(BF16)
        if d == 4:
            send(out, met_in.at[half, h, 1], at(2 if h == 0 else -2), ("met", half, h, h), "output")
        elif abs(d) == 3:
            send(out, met_in.at[half, side, 0 if h == side else 2], at(1 if d > 0 else -1), ("met", half, side, h), "output")
        elif abs(d) == 2 and h != side:
            send(out, met_in.at[half, side, 3], at(1 if d > 0 else -1), ("near", half, side), "output")
        else:
            send(out, fin.at[half, ENDS.index((d, h))], at(d, h), ("ended", half), "output")

    def steps(k, *which):
        for half in (0, 1):
            if k is not None:
                arrived(sib_in.at[k, half], "handed", k, half)
            for d, h in which:
                step(d, h, half)

    X, C = 0, 1
    pass_on(X, 1, 0)
    own_pair(X)
    pass_on(C, 1, 0)
    own_pair(C)
    pass_on(X, 1, 2)
    pass_on(X, 2, 0)
    partial_sums(0)
    pass_on(C, 1, 2)
    pass_on(C, 2, 0)
    pass_on(X, 2, 2)
    pass_on(X, 3, 0)
    pass_on(C, 2, 2)
    partial_sums(1)
    pass_on(C, 3, 0)
    pass_on(X, 3, 2)
    pass_on(X, 4, 0)
    pass_on(C, 3, 2)
    mix_sums(0)
    pass_on(C, 4, 0)
    pass_on(X, 4, 2)
    partial_sums(2)
    pass_on(C, 4, 2)
    partial_sums(3)
    finish_units(2)
    finish_units(3)
    finish_units(1)
    finish_units(0)
    output_terms(2)
    output_terms(3)
    steps(2, (3, 1), (-3, 0))
    steps(3, (4, 0), (4, 1), (3, 0), (-3, 1))
    output_terms(1)
    steps(None, (2, 1))
    steps(1, (-1, 1), (-2, 0))
    output_terms(0)
    steps(None, (1, 1))
    steps(0, (0, 1), (1, 0))
    steps(None, (2, 0), (-2, 1))
    steps(None, (-1, 0))

    arrived(hs, "lent")
    rows_all = CHUNKS * chunk
    half_width = width // 2
    tile = 256
    here = pl.multiple_of(core * units, units)
    there = pl.multiple_of((1 - core) * units, units)
    stores = []
    for m, values in enumerate((cg, xg, xg)):

        def weight_tile(i, carry):
            at_col = pl.multiple_of(core * half_width + i * tile, tile)
            at_row = pl.multiple_of(i * tile, tile)
            left = values[:, pl.ds(at_col, tile)]
            for source, place in ((hh, here), (hs, there)):
                right = source[:, :, :, :, m * units : (m + 1) * units].reshape(rows_all, units)
                gw[m, pl.ds(at_row, tile), pl.ds(place, units)] = dot_rows(left, right).astype(BF16)
            return carry

        lax.fori_loop(0, half_width // tile, weight_tile, 0)
        stores.append(pltpu.make_async_copy(gw.at[m], gw_out.at[m], osem.at[m]))
        stores[m].start()

    for half, out_ref in enumerate((lo_ref, tg_ref)):
        arrived(fin.at[half], "ended", half)
        total = mine[0, half, 0] + sib_in[0, half, 0].astype(F32)
        for place in range(len(ENDS)):
            total = total + fin[half, place].astype(F32)
        out_ref[...] = total.astype(BF16)
    for a in (0, 1):
        left(xg.at[pl.ds(0, 31 * tokens), :], f"gather{a}")
    two = pl.ds(0, CHUNKS - len(DIRECT))
    left(in_y.at[two], "sums y")
    left(in_x.at[two], "sums x")
    left(end_x.at[two], "mixed x")
    left(end_y.at[two], "mixed y")
    left(got, "sums")
    left(hh.at[:, pl.ds(0, 3), :], "spread")
    left(hh.at[:, 0, 0], "spread last")
    left(hs, "lent")
    left(sib_in, "handed")
    left(xg.at[pl.ds(0, 30 * tokens), :], "output")
    for store in stores:
        store.wait()
    kinds = [kind for kind, _ in places]
    assert (kinds.count("send"), kinds.count("recv")) == (SENDS, RECEIVES)


def store_results(lo, tg, gw, lo_out, tg_out, gate_out, up_out, down_out, stage, small, in_sem, out_sem):
    rows = gw.shape[1] // 2
    moves = []
    for m, out in enumerate((down_out, gate_out, up_out)):
        for i in range(2):
            part = pl.ds(i * rows, rows)
            moves.append((gw.at[m, part], stage.at[m, part], out.at[part]))
    moves += [(lo, small.at[0], lo_out), (tg, small.at[1], tg_out)]
    loads = [pltpu.make_async_copy(src, via, in_sem.at[n]) for n, (src, via, _) in enumerate(moves)]
    stores = [pltpu.make_async_copy(via, dst, out_sem.at[n]) for n, (_, via, dst) in enumerate(moves)]
    for load in loads:
        load.start()
    for load, store in zip(loads, stores):
        load.wait()
        store.start()
    for store in stores:
        store.wait()


def shards(layer_input, out_cotangent, old_gate, old_up, old_down):
    tokens, width = layer_input.shape
    units = old_gate.shape[1]
    all_tokens = 32 * tokens
    vmem = pl.BlockSpec(memory_space=pltpu.VMEM)
    hbm = pl.BlockSpec(memory_space=pltpu.HBM)
    grad_shape = jax.ShapeDtypeStruct((width // 2, 2 * units), BF16)
    out_shape = jax.ShapeDtypeStruct((tokens, width), BF16)
    results = pl.pallas_call(
        kernel,
        out_shape=(out_shape, out_shape, jax.ShapeDtypeStruct((3,) + grad_shape.shape, BF16)),
        in_specs=[hbm] * 5,
        out_specs=[vmem, vmem, hbm],
        scratch_shapes=[
            pltpu.VMEM((width, units), BF16),
            pltpu.VMEM((width, units), BF16),
            pltpu.VMEM((width, units), BF16),
            pltpu.VMEM((all_tokens, width), BF16),
            pltpu.VMEM((all_tokens, width), BF16),
            pltpu.VMEM((CHUNKS, 4, 2, tokens, 3 * units), BF16),
            pltpu.VMEM((CHUNKS, 3, 2, tokens, CUT), BF16),
            pltpu.VMEM((CHUNKS, 4, tokens, 3 * units - CUT), BF16),
            pltpu.VMEM((CHUNKS, tokens, CUT), BF16),
            pltpu.VMEM((CHUNKS, 4, tokens, 3 * units - CUT), BF16),
            pltpu.VMEM((CHUNKS, 3, tokens, 3 * units - CUT), BF16),
            pltpu.VMEM((CHUNKS, tokens, CUT), BF16),
            pltpu.VMEM((CHUNKS, tokens, CUT), F32),
            pltpu.VMEM((len(DIRECT), 7, tokens, 3 * units), BF16),
            pltpu.VMEM((CHUNKS, 4, 2, tokens, 3 * units), BF16),
            pltpu.VMEM((CHUNKS, 4, 2, tokens, 3 * units), BF16),
            pltpu.VMEM((CHUNKS, 2, 4, tokens, width), F32),
            pltpu.VMEM((CHUNKS, 2, 4, tokens, width), BF16),
            pltpu.VMEM((CHUNKS, 2, 4, tokens, width), BF16),
            pltpu.VMEM((2, 16, tokens, width), BF16),
            pltpu.VMEM((2, 2, 4, tokens, width), BF16),
            pltpu.VMEM((2, len(ENDS), tokens, width), BF16),
            pltpu.VMEM((3, width // 2, 2 * units), BF16),
            pltpu.SemaphoreType.DMA((5,)),
            pltpu.SemaphoreType.DMA((3,)),
            pltpu.SemaphoreType.DMA((SENDS,)),
            pltpu.SemaphoreType.DMA((RECEIVES,)),
        ],
        compiler_params=pltpu.CompilerParams(
            collective_id=0, has_side_effects=True, vmem_limit_bytes=63 * 1024 * 1024
        ),
        cost_estimate=pl.CostEstimate(
            flops=18 * all_tokens * width * units, bytes_accessed=12 * width * units, transcendentals=0
        ),
    )(layer_input, out_cotangent, old_gate, old_up, old_down)
    return pl.pallas_call(
        store_results,
        out_shape=(out_shape, out_shape, grad_shape, grad_shape, grad_shape),
        in_specs=[hbm] * 3,
        out_specs=[hbm] * 5,
        scratch_shapes=[
            pltpu.VMEM((3,) + grad_shape.shape, BF16),
            pltpu.VMEM((2,) + out_shape.shape, BF16),
            pltpu.SemaphoreType.DMA((8,)),
            pltpu.SemaphoreType.DMA((8,)),
        ],
        compiler_params=pltpu.CompilerParams(vmem_limit_bytes=63 * 1024 * 1024),
    )(*results)


def solution(mesh):
    wide = P("dp", "tensor")
    stored = P("tensor", "dp")
    return jax.shard_map(
        shards,
        mesh=mesh,
        in_specs=(wide, wide, stored, stored, stored),
        out_specs=(wide, wide, stored, stored, stored),
        check_vma=False,
    )
```

```python
import jax
import jax.numpy as jnp
from jax import lax
from jax.experimental import pallas as pl
from jax.experimental.pallas import tpu as pltpu
from jax.sharding import PartitionSpec as P

MESH = pl.DeviceIdType.MESH
F32 = jnp.float32
BF16 = jnp.bfloat16

ENTRIES = (
    (0, 0), (0, 1), (1, 0), (-1, 0),
    (1, 1), (-1, 1), (2, 0), (-2, 0),
    (2, 1), (-2, 1), (3, 1), (-3, 0),
    (3, 0), (-3, 1), (4, 0), (4, 1),
)
CHUNKS = 4
DIRECT = (1, 2, 3)
SENDS, RECEIVES = 12, 30 + 8 + 4 * (CHUNKS - len(DIRECT)) + len(DIRECT) + 23
CUT = 640
FIRST, SECOND = pl.ds(0, CUT), pl.ds(CUT, 1536 - CUT)
ENDS = ((2, 0), (-2, 1), (1, 0), (1, 1), (-1, 0), (-1, 1), (0, 1))


def dot(a, b):
    return jnp.dot(a, b, preferred_element_type=F32)


def dot_cols(a, b):
    return lax.dot_general(a, b, (((1,), (1,)), ((), ())), preferred_element_type=F32)


def dot_rows(a, b):
    return lax.dot_general(a, b, (((0,), (0,)), ((), ())), preferred_element_type=F32)


def kernel(
    x_ref, c_ref, wg_any, wu_any, wd_any,
    lo_ref, tg_ref, gw_out,
    wg, wu, wd, xg, cg, part, in_x, in_y, out_x, out_y, end_x, end_y, kept, got, hh, hs, mine, sib_out, sib_in, sums_out, met_in, fin, gw,
    wsem, osem, ssem, rsem,
):
    dp = lax.axis_index("dp")
    me = lax.axis_index("tensor")
    core, yh, z = dp % 2, (dp // 2) % 2, dp // 4
    x, yl = me // 2, me % 2
    tokens, width = x_ref.shape
    units = wg_any.shape[1]
    chunk = 8 * tokens

    def at(dz, flip_y=0, flip_core=0):
        return (((z + dz + 8) % 8) * 4 + ((yh + flip_y) % 2) * 2 + (core + flip_core) % 2, me)

    def x_of(j):
        return (x, x + 1 - 2 * (x % 2), (x + 2) % 4, 3 - x)[j]

    def peer_of(j):
        return (dp, x_of(j // 2) * 2 + (yl + j % 2) % 2)

    def x_peer(j):
        return peer_of(2 * j)

    y_peer = peer_of(1)
    sibling = at(0, 0, 1)
    loads = [
        pltpu.make_async_copy(src, dst, wsem.at[i])
        for i, (src, dst) in enumerate(((wg_any, wg), (wu_any, wu), (wd_any, wd)))
    ]
    mine_in = [
        pltpu.make_async_copy(src, dst.at[pl.ds(0, tokens), :], wsem.at[3 + i])
        for i, (src, dst) in enumerate(((x_ref, xg), (c_ref, cg)))
    ]
    for load in mine_in + loads:
        load.start()

    barrier = pltpu.get_barrier_semaphore()
    peers = [at(1), at(-1), at(1, 1), at(-1, 1), at(0, 1), sibling]
    peers += [at(2), at(-2), at(2, 1), at(-2, 1)]
    peers += [peer_of(j) for j in range(1, 8)]
    for peer in peers:
        pl.semaphore_signal(barrier, inc=1, device_id=peer, device_id_type=MESH)
    pl.semaphore_wait(barrier, len(peers))

    places = {}

    def place_of(kind, key):
        return places.setdefault((kind, key), sum(1 for k, _ in places if k == kind))

    def send(src, dst, device, key, group):
        copy = pltpu.make_async_remote_copy(
            src_ref=src, dst_ref=dst, send_sem=ssem.at[place_of("send", group)], recv_sem=rsem.at[place_of("recv", key)],
            device_id=device, device_id_type=MESH,
        )
        copy.start()

    def of_size(ref, key, group):
        return pltpu.make_async_remote_copy(
            src_ref=ref, dst_ref=ref, send_sem=ssem.at[place_of("send", group)], recv_sem=rsem.at[place_of("recv", key)],
            device_id=sibling, device_id_type=MESH,
        )

    def arrived(ref, *key):
        of_size(ref, key, "gather0").wait_recv()

    def left(ref, group):
        of_size(ref, ("gather", 0, 1, 0), group).wait_send()

    held = (xg, cg)
    own = (x_ref, c_ref)

    def block(a, d, s):
        return held[a].at[pl.ds((ENTRIES.index((d, s // 2)) * 2 + s % 2) * tokens, tokens), :]

    def pass_to(a, src, d, s, device):
        send(src, block(a, d, s), device, ("gather", a, d, s), f"gather{a}")

    def share(a, src, d, s):
        send(src, block(a, d, s + 1), sibling, ("share", ENTRIES.index((d, s // 2)) // 4), f"gather{a}")

    def here_now(a, d, s):
        arrived(block(a, d, s), "gather", a, d, s)

    for a in (0, 1):
        pass_to(a, own[a], -1, 0, at(1))
        pass_to(a, own[a], 1, 0, at(-1))
        pass_to(a, own[a], -1, 2, at(1, 1))
        pass_to(a, own[a], 1, 2, at(-1, 1))
        pass_to(a, own[a], 0, 2, at(0, 1))
        share(a, own[a], 0, 0)

    def pass_on(a, d, s):
        for way in (1, -1):
            to = -way * d if d < 4 else 4
            if d == 4 and (way > 0) != (s == 0):
                continue
            here_now(a, to, s)
            if d < 3:
                pass_to(a, block(a, to, s), to - way, s, at(way))
            elif d == 3 and (way > 0) == (s == 0):
                pass_to(a, block(a, to, s), 4, s, at(way))
            share(a, block(a, to, s), to, s)

    def own_pair(a):
        here_now(a, 0, 2)
        share(a, block(a, 0, 2), 0, 2)

    def partial_sums(k):
        rows = pl.ds(k * chunk, chunk)
        arrived(xg.at[rows, :], "share", k)
        if k == 0:
            for load in mine_in + loads:
                load.wait()
        for i, (values, weight) in enumerate(((xg, wg), (xg, wu), (cg, wd))):
            sums = dot(values[rows, :], weight[...]).astype(BF16)
            part[k, :, :, :, i * units : (i + 1) * units] = sums.reshape(4, 2, tokens, units)
        if k in DIRECT:
            for j in (5, 4, 7, 3, 6, 2, 1):
                src = part.at[k, x_of(j // 2), (yl + j % 2) % 2]
                send(src, got.at[DIRECT.index(k), j - 1], peer_of(j), ("sums", k), "sums")
            return
        send(part.at[k, :, 1 - yl, :, SECOND], in_y.at[k], y_peer, ("sums y", k), "sums y")
        for j in (2, 1, 3):
            send(part.at[k, x_of(j), :, :, FIRST], in_x.at[k, j - 1], x_peer(j), ("sums x", k), "sums x")

    def mix_sums(k):
        arrived(in_y.at[k], "sums y", k)
        both = part[k, :, yl, :, SECOND].astype(F32) + in_y[k].astype(F32)
        out_y[k] = both.astype(BF16)
        for j in (2, 1, 3):
            send(out_y.at[k, x_of(j)], end_x.at[k, j - 1], x_peer(j), ("mixed x", k), "mixed x")
        arrived(in_x.at[k], "sums x", k)
        theirs, ours = part[k, x, 1 - yl, :, FIRST].astype(F32), part[k, x, yl, :, FIRST].astype(F32)
        for j in range(3):
            theirs = theirs + in_x[k, j, 1 - yl].astype(F32)
            ours = ours + in_x[k, j, yl].astype(F32)
        out_x[k] = theirs.astype(BF16)
        kept[k] = ours
        send(out_x.at[k], end_y.at[k], y_peer, ("mixed y", k), "mixed y")

    def finish_units(k):
        if k in DIRECT:
            mail = got.at[DIRECT.index(k)]
            arrived(mail, "sums", k)
            total = part[k, x, yl].astype(F32)
            for j in range(7):
                total = total + mail[j].astype(F32)
        else:
            arrived(end_x.at[k], "mixed x", k)
            arrived(end_y.at[k], "mixed y", k)
            first = kept[k] + end_y[k].astype(F32)
            second = out_y[k, x].astype(F32)
            for j in range(3):
                second = second + end_x[k, j].astype(F32)
            total = jnp.concatenate([first, second], axis=1)
        gate, up, grad = (total[:, i * units : (i + 1) * units] for i in range(3))
        sigma = jax.nn.sigmoid(gate)
        silu = gate * sigma
        slope = sigma * (1.0 + gate * (1.0 - sigma))
        mine_now = hh.at[k, x, yl]
        mine_now[:, 0:units] = (silu * up).astype(BF16)
        mine_now[:, units : 2 * units] = (grad * up * slope).astype(BF16)
        mine_now[:, 2 * units :] = (grad * silu).astype(BF16)
        for j in (5, 4, 7, 3, 6, 2, 1):
            send(mine_now, mine_now, peer_of(j), ("spread", k), "spread last" if j == 1 else "spread")

    def output_terms(k):
        arrived(got.at[0], "spread", k)
        send(hh.at[k, :, 0], hs.at[k, :, 1], sibling, ("lent",), "lent")
        send(hh.at[k, :, 1], hs.at[k, :, 0], sibling, ("lent",), "lent")
        values = hh[k].reshape(chunk, 3 * units)
        for half in (0, 1):
            if half == 0:
                term = dot_cols(values[:, 0:units], wd[...])
            else:
                term = dot_cols(values[:, units : 2 * units], wg[...])
                term = term + dot_cols(values[:, 2 * units :], wu[...])
            term = term.reshape(4, 2, tokens, width)
            mine[k, half] = term[:, 0]
            sib_out[k, half] = term[:, 1].astype(BF16)
            send(sib_out.at[k, half], sib_in.at[k, half], sibling, ("handed", k, half), "handed")

    def step(d, h, half):
        entry = ENTRIES.index((d, h))
        value = mine[entry // 4, half, entry % 4] + sib_in[entry // 4, half, entry % 4].astype(F32)
        side = 0 if d > 0 else 1
        out = sums_out.at[half, entry]
        if abs(d) == 2 and h == side:
            arrived(met_in.at[half, side, pl.ds(0, 2)], "met", half, side, h)
            value = value + met_in[half, side, 0].astype(F32) + met_in[half, side, 1].astype(F32)
        elif abs(d) == 2:
            arrived(met_in.at[half, side, 2], "met", half, side, h)
            value = value + met_in[half, side, 2].astype(F32)
        elif abs(d) == 1 and h != side:
            arrived(met_in.at[half, side, 3], "near", half, side)
            value = value + met_in[half, side, 3].astype(F32)
        out[...] = value.astype(BF16)
        if d == 4:
            send(out, met_in.at[half, h, 1], at(2 if h == 0 else -2), ("met", half, h, h), "output")
        elif abs(d) == 3:
            send(out, met_in.at[half, side, 0 if h == side else 2], at(1 if d > 0 else -1), ("met", half, side, h), "output")
        elif abs(d) == 2 and h != side:
            send(out, met_in.at[half, side, 3], at(1 if d > 0 else -1), ("near", half, side), "output")
        else:
            send(out, fin.at[half, ENDS.index((d, h))], at(d, h), ("ended", half), "output")

    def steps(k, *which):
        for half in (0, 1):
            if k is not None:
                arrived(sib_in.at[k, half], "handed", k, half)
            for d, h in which:
                step(d, h, half)

    X, C = 0, 1
    pass_on(X, 1, 0)
    own_pair(X)
    pass_on(C, 1, 0)
    own_pair(C)
    pass_on(X, 1, 2)
    pass_on(X, 2, 0)
    partial_sums(0)
    pass_on(C, 1, 2)
    pass_on(C, 2, 0)
    pass_on(X, 2, 2)
    partial_sums(1)
    pass_on(X, 3, 0)
    pass_on(C, 2, 2)
    pass_on(C, 3, 0)
    pass_on(X, 3, 2)
    pass_on(X, 4, 0)
    pass_on(C, 3, 2)
    mix_sums(0)
    pass_on(C, 4, 0)
    pass_on(X, 4, 2)
    partial_sums(2)
    pass_on(C, 4, 2)
    partial_sums(3)
    finish_units(2)
    finish_units(3)
    finish_units(1)
    finish_units(0)
    output_terms(2)
    output_terms(3)
    steps(2, (3, 1), (-3, 0))
    steps(3, (3, 0), (-3, 1), (4, 0), (4, 1))
    output_terms(1)
    steps(None, (2, 1))
    steps(1, (-2, 0), (-1, 1))
    output_terms(0)
    steps(None, (1, 1))
    steps(0, (0, 1), (1, 0))
    steps(None, (2, 0), (-2, 1))
    steps(None, (-1, 0))

    arrived(hs, "lent")
    rows_all = CHUNKS * chunk
    half_width = width // 2
    tile = 256
    here = pl.multiple_of(core * units, units)
    there = pl.multiple_of((1 - core) * units, units)
    stores = []
    for m, values in enumerate((cg, xg, xg)):

        def weight_tile(i, carry):
            at_col = pl.multiple_of(core * half_width + i * tile, tile)
            at_row = pl.multiple_of(i * tile, tile)
            left = values[:, pl.ds(at_col, tile)]
            for source, place in ((hh, here), (hs, there)):
                right = source[:, :, :, :, m * units : (m + 1) * units].reshape(rows_all, units)
                gw[m, pl.ds(at_row, tile), pl.ds(place, units)] = dot_rows(left, right).astype(BF16)
            return carry

        lax.fori_loop(0, half_width // tile, weight_tile, 0)
        stores.append(pltpu.make_async_copy(gw.at[m], gw_out.at[m], osem.at[m]))
        stores[m].start()

    for half, out_ref in enumerate((lo_ref, tg_ref)):
        arrived(fin.at[half], "ended", half)
        total = mine[0, half, 0] + sib_in[0, half, 0].astype(F32)
        for place in range(len(ENDS)):
            total = total + fin[half, place].astype(F32)
        out_ref[...] = total.astype(BF16)
    for a in (0, 1):
        left(xg.at[pl.ds(0, 31 * tokens), :], f"gather{a}")
    two = pl.ds(0, CHUNKS - len(DIRECT))
    left(in_y.at[two], "sums y")
    left(in_x.at[two], "sums x")
    left(end_x.at[two], "mixed x")
    left(end_y.at[two], "mixed y")
    left(got, "sums")
    left(hh.at[:, pl.ds(0, 3), :], "spread")
    left(hh.at[:, 0, 0], "spread last")
    left(hs, "lent")
    left(sib_in, "handed")
    left(xg.at[pl.ds(0, 30 * tokens), :], "output")
    for store in stores:
        store.wait()
    kinds = [kind for kind, _ in places]
    assert (kinds.count("send"), kinds.count("recv")) == (SENDS, RECEIVES)


def store_results(lo, tg, gw, lo_out, tg_out, gate_out, up_out, down_out, stage, small, in_sem, out_sem):
    rows = gw.shape[1] // 2
    moves = []
    for m, out in enumerate((down_out, gate_out, up_out)):
        for i in range(2):
            part = pl.ds(i * rows, rows)
            moves.append((gw.at[m, part], stage.at[m, part], out.at[part]))
    moves += [(lo, small.at[0], lo_out), (tg, small.at[1], tg_out)]
    loads = [pltpu.make_async_copy(src, via, in_sem.at[n]) for n, (src, via, _) in enumerate(moves)]
    stores = [pltpu.make_async_copy(via, dst, out_sem.at[n]) for n, (_, via, dst) in enumerate(moves)]
    for load in loads:
        load.start()
    for load, store in zip(loads, stores):
        load.wait()
        store.start()
    for store in stores:
        store.wait()


def shards(layer_input, out_cotangent, old_gate, old_up, old_down):
    tokens, width = layer_input.shape
    units = old_gate.shape[1]
    all_tokens = 32 * tokens
    vmem = pl.BlockSpec(memory_space=pltpu.VMEM)
    hbm = pl.BlockSpec(memory_space=pltpu.HBM)
    grad_shape = jax.ShapeDtypeStruct((width // 2, 2 * units), BF16)
    out_shape = jax.ShapeDtypeStruct((tokens, width), BF16)
    results = pl.pallas_call(
        kernel,
        out_shape=(out_shape, out_shape, jax.ShapeDtypeStruct((3,) + grad_shape.shape, BF16)),
        in_specs=[hbm] * 5,
        out_specs=[vmem, vmem, hbm],
        scratch_shapes=[
            pltpu.VMEM((width, units), BF16),
            pltpu.VMEM((width, units), BF16),
            pltpu.VMEM((width, units), BF16),
            pltpu.VMEM((all_tokens, width), BF16),
            pltpu.VMEM((all_tokens, width), BF16),
            pltpu.VMEM((CHUNKS, 4, 2, tokens, 3 * units), BF16),
            pltpu.VMEM((CHUNKS, 3, 2, tokens, CUT), BF16),
            pltpu.VMEM((CHUNKS, 4, tokens, 3 * units - CUT), BF16),
            pltpu.VMEM((CHUNKS, tokens, CUT), BF16),
            pltpu.VMEM((CHUNKS, 4, tokens, 3 * units - CUT), BF16),
            pltpu.VMEM((CHUNKS, 3, tokens, 3 * units - CUT), BF16),
            pltpu.VMEM((CHUNKS, tokens, CUT), BF16),
            pltpu.VMEM((CHUNKS, tokens, CUT), F32),
            pltpu.VMEM((len(DIRECT), 7, tokens, 3 * units), BF16),
            pltpu.VMEM((CHUNKS, 4, 2, tokens, 3 * units), BF16),
            pltpu.VMEM((CHUNKS, 4, 2, tokens, 3 * units), BF16),
            pltpu.VMEM((CHUNKS, 2, 4, tokens, width), F32),
            pltpu.VMEM((CHUNKS, 2, 4, tokens, width), BF16),
            pltpu.VMEM((CHUNKS, 2, 4, tokens, width), BF16),
            pltpu.VMEM((2, 16, tokens, width), BF16),
            pltpu.VMEM((2, 2, 4, tokens, width), BF16),
            pltpu.VMEM((2, len(ENDS), tokens, width), BF16),
            pltpu.VMEM((3, width // 2, 2 * units), BF16),
            pltpu.SemaphoreType.DMA((5,)),
            pltpu.SemaphoreType.DMA((3,)),
            pltpu.SemaphoreType.DMA((SENDS,)),
            pltpu.SemaphoreType.DMA((RECEIVES,)),
        ],
        compiler_params=pltpu.CompilerParams(
            collective_id=0, has_side_effects=True, vmem_limit_bytes=63 * 1024 * 1024
        ),
        cost_estimate=pl.CostEstimate(
            flops=18 * all_tokens * width * units, bytes_accessed=12 * width * units, transcendentals=0
        ),
    )(layer_input, out_cotangent, old_gate, old_up, old_down)
    return pl.pallas_call(
        store_results,
        out_shape=(out_shape, out_shape, grad_shape, grad_shape, grad_shape),
        in_specs=[hbm] * 3,
        out_specs=[hbm] * 5,
        scratch_shapes=[
            pltpu.VMEM((3,) + grad_shape.shape, BF16),
            pltpu.VMEM((2,) + out_shape.shape, BF16),
            pltpu.SemaphoreType.DMA((8,)),
            pltpu.SemaphoreType.DMA((8,)),
        ],
        compiler_params=pltpu.CompilerParams(vmem_limit_bytes=63 * 1024 * 1024),
    )(*results)


def solution(mesh):
    wide = P("dp", "tensor")
    stored = P("tensor", "dp")
    return jax.shard_map(
        shards,
        mesh=mesh,
        in_specs=(wide, wide, stored, stored, stored),
        out_specs=(wide, wide, stored, stored, stored),
        check_vma=False,
    )
```
